32 devices in a mesh: seq: 16 (over z, x, core), fsdp: 2 (over y).
Axes of the slice: x: 2, y: 2, z: 4, core: 2. Of those that a mesh axis runs over, the one named last changes fastest.
Arguments:
- block_input: bfloat16 [8, 8192, 768], P('fsdp', 'seq'), may hold values from -6 to 6
- gain_before: bfloat16 [768], P(('seq', 'fsdp')), may hold values from 0.5 to 1.5
- joint_weight: bfloat16 [768, 2304], P(('seq', 'fsdp')), may hold values from -0.21875 to 0.21875
- mixing_weight: bfloat16 [768, 768], P(('seq', 'fsdp')), may hold values from -1.25 to 1.25
- gain_middle: bfloat16 [768], P(('seq', 'fsdp')), may hold values from 0.5 to 1.5
- expand_weight: bfloat16 [768, 2304], P(('seq', 'fsdp')), may hold values from -0.21875 to 0.21875
- reduce_weight: bfloat16 [1152, 768], P(None, ('seq', 'fsdp')), may hold values from -0.25 to 0.25
- upstream: bfloat16 [8, 8192, 768], P('fsdp', 'seq'), may hold values from -8 to 8
Outputs:
- block_output: bfloat16 [8, 8192, 768], P('fsdp', 'seq')
- input_grad: float32 [8, 8192, 768], P('fsdp', 'seq')
- before_grad: float32 [768], P(('seq', 'fsdp'))
- joint_grad: float32 [768, 2304], P(('seq', 'fsdp'))
- mixing_grad: float32 [768, 768], P(('seq', 'fsdp'))
- middle_grad: float32 [768], P(('seq', 'fsdp'))
- expand_grad: float32 [768, 2304], P(('seq', 'fsdp'))
- reduce_grad: float32 [1152, 768], P(None, ('seq', 'fsdp'))
The draws below stay inside these ranges and needn't reach their ends.
All inputs are finite; a program needn't handle non-finite values.
Results may differ from the reference program's by a relative error of at most 0.015.
Values may be sent and summed in bfloat16 or wider, within the bound.
A program may use at most 256 MiB of HBM per device.

```python
import math
import jax
import jax.numpy as jnp
from jax import lax

D = 768
HEADS = 12
HEAD_DIM = 64
FF = 1152
REACH = 64
SEQ_LEN = 8192
SEQS = 8


def raised(values, stream_key, source, target, shards_of, factor):
    def block_of(position):
        return (jnp.arange(values.shape[position]) // (values.shape[position] // shards_of)).reshape((-1,) + (1,) * (values.ndim - 1 - position))

    one_side = jax.random.permutation(stream_key, shards_of)[block_of(target)]
    second = (block_of(target) + shards_of // 2) % shards_of
    return jnp.where((block_of(source) == one_side) | (block_of(source) == second), factor * values, values)


def block_levels(key, dims, split, least, top_value):
    def one(dim, parts):
        heights = jax.random.uniform(jax.random.fold_in(jax.random.fold_in(key, 6), dim), (parts,), jnp.float32, least / len(split), top_value / len(split))
        return jnp.repeat(jnp.exp(heights), dims[dim] // parts).reshape((-1,) + (1,) * (len(dims) - dim - 1))

    factor_of = one(*split[0])
    for cut in split[1:]:
        factor_of = factor_of * one(*cut)
    return factor_of


def normal_values(rng, extent, scale, limit, shards=(), held_as=jnp.bfloat16):
    level = block_levels(rng, extent, shards, -0.22, 0.18) if shards else 1.0
    entries = jax.random.normal(rng, extent, jnp.float32) * scale * level
    return jnp.minimum(jnp.maximum(entries, -limit), limit).astype(held_as)


def gaussian_with(rng, extent, deviation, reach, shards, heavy, held_as=jnp.bfloat16):
    drawn = deviation * jax.random.normal(rng, extent, jnp.float32)
    if shards:
        drawn = drawn * block_levels(rng, extent, shards, -0.22, 0.18)
    return jnp.clip(raised(drawn, jax.random.fold_in(rng, 3), *heavy), -reach, reach).astype(held_as)


def setup_inputs(seed: int = 0) -> dict:
    splits = jax.random.split(jax.random.key(seed), 9)
    return {
        "block_input": normal_values(splits[0], (SEQS, SEQ_LEN, D), 1.0, 6.0, ((0, 2), (1, 16))),
        "gain_before": jnp.clip(1.0 + 0.1 * jax.random.normal(splits[1], (D,), jnp.float32), 0.5, 1.5).astype(jnp.bfloat16),
        "joint_weight": normal_values(splits[2], (D, 3 * D), D ** -0.5, 0.21875, ((0, 32),)),
        "mixing_weight": normal_values(splits[3], (D, D), (D // 32) ** -0.5, 1.25, ((0, 32),)),
        "gain_middle": jnp.clip(1.0 + 0.1 * jax.random.normal(splits[4], (D,), jnp.float32), 0.5, 1.5).astype(jnp.bfloat16),
        "expand_weight": normal_values(splits[5], (D, 2 * FF), D ** -0.5, 0.21875, ((0, 32),)),
        "reduce_weight": normal_values(splits[6], (FF, D), (FF // 2) ** -0.5, 0.25, ((1, 32),)),
        "upstream": gaussian_with(splits[7], (SEQS, SEQ_LEN, D), 1.0, 8.0, ((0, 2), (1, 16)), (1, 2, 16, 2.0)),
    }


epsilon = 1e-05
masked_value = -1e+30

@jax.custom_vjp
def low(v):
    return lax.optimization_barrier(v.astype(jnp.bfloat16)).astype(jnp.float32)

@jax.custom_vjp
def low_back(v):
    return v

def low_keep(v):
    return (low(v), None)

def low_pass(kept, grad):
    return (grad,)

def back_keep(v):
    return (v, None)

def back_low(kept, grad):
    return (low(grad),)
low.defvjp(low_keep, low_pass)
low_back.defvjp(back_keep, back_low)

def layer_norm(values, gain_row):
    center = values - lax.optimization_barrier(jnp.mean(values, axis=-1, keepdims=True))
    spread = lax.optimization_barrier(jnp.mean(center * center, axis=-1, keepdims=True))
    return center * lax.rsqrt(spread + epsilon) * gain_row

def rotary_tables(positions, head_size):
    half_dim = head_size // 2
    exponent = jnp.arange(half_dim, dtype=jnp.float32) * (2.0 / head_size)
    inverse = jnp.power(10000.0, -exponent)
    angles = positions.astype(jnp.float32)[:, None] * inverse[None, :]
    full_angles = jnp.concatenate([angles, angles], axis=-1)
    return (jnp.cos(full_angles), jnp.sin(full_angles))

def rotate(values, cosine_table, sine_table):
    half_dim = values.shape[-1] // 2
    turned = jnp.concatenate([-values[..., half_dim:], values[..., :half_dim]], axis=-1)
    return values * cosine_table[:, None, :] + turned * sine_table[:, None, :]

def attention_sequence(queries, key_rows, value_rows):
    length = queries.shape[0]
    block_rows = min(512, length)
    block_count = length // block_rows
    highest = lax.Precision.HIGHEST
    factor = 1.0 / math.sqrt(HEAD_DIM)
    padded_keys = jnp.pad(key_rows, ((REACH, REACH), (0, 0), (0, 0)))
    padded_values = jnp.pad(value_rows, ((REACH, REACH), (0, 0), (0, 0)))

    def one_block(index):
        start = index * block_rows
        query_part = lax.dynamic_slice_in_dim(queries, start, block_rows, 0)
        key_part = lax.dynamic_slice_in_dim(padded_keys, start, block_rows + 2 * REACH, 0)
        value_part = lax.dynamic_slice_in_dim(padded_values, start, block_rows + 2 * REACH, 0)
        scores = low_back(jnp.einsum('qhd,khd->hqk', query_part, key_part, precision=highest) * factor)
        query_pos = start + jnp.arange(block_rows, dtype=jnp.int32)
        key_pos = start - REACH + jnp.arange(block_rows + 2 * REACH, dtype=jnp.int32)
        allowed = (jnp.abs(query_pos[:, None] - key_pos[None, :]) <= REACH) & (key_pos[None, :] >= 0) & (key_pos[None, :] < length)
        scores = jnp.where(allowed[None], scores, masked_value)
        maxima = lax.optimization_barrier(jnp.max(scores, axis=-1, keepdims=True))
        exponent_terms = jnp.exp(scores - maxima)
        probs = low(exponent_terms / lax.optimization_barrier(jnp.sum(exponent_terms, axis=-1, keepdims=True)))
        return jnp.einsum('hqk,khd->qhd', probs, value_part, precision=highest)
    outputs = lax.map(jax.checkpoint(one_block), jnp.arange(block_count, dtype=jnp.int32))
    return outputs.reshape(length, HEADS, HEAD_DIM)

def forward_sequence(inputs, gain_before, joint_weight, mixing_weight, gain_middle, expand_weight, reduce_weight):
    length = inputs.shape[0]
    highest = lax.Precision.HIGHEST
    normed_attn = low(layer_norm(inputs, gain_before))
    joint_out = low_back(jnp.dot(normed_attn, joint_weight, precision=highest))
    queries = joint_out[:, :D].reshape(length, HEADS, HEAD_DIM)
    key_rows = joint_out[:, D:2 * D].reshape(length, HEADS, HEAD_DIM)
    value_rows = joint_out[:, 2 * D:].reshape(length, HEADS, HEAD_DIM)
    cosine_table, sine_table = rotary_tables(jnp.arange(length, dtype=jnp.int32), HEAD_DIM)
    query_rot = low(rotate(queries, cosine_table, sine_table))
    key_rot = low(rotate(key_rows, cosine_table, sine_table))
    value_low = low(value_rows)
    context = attention_sequence(query_rot, key_rot, value_low)
    context = low(low_back(context.reshape(length, D)))
    middle = inputs + low_back(jnp.dot(context, mixing_weight, precision=highest))
    normed_ffn = low(layer_norm(middle, gain_middle))
    expanded = low_back(jnp.dot(normed_ffn, expand_weight, precision=highest))
    hidden = low(jax.nn.gelu(expanded[:, :FF], approximate=False) * expanded[:, FF:])
    return middle + low_back(jnp.dot(hidden, reduce_weight, precision=highest))

def reference(block_input, gain_before, joint_weight, mixing_weight, gain_middle, expand_weight, reduce_weight, upstream):
    params = tuple((matrix.astype(jnp.float32) for matrix in (gain_before, joint_weight, mixing_weight, gain_middle, expand_weight, reduce_weight)))

    def scan_step(totals, inputs_pair):
        seq_input, seq_upstream = inputs_pair
        outputs, pullback = jax.vjp(forward_sequence, seq_input.astype(jnp.float32), *params)
        gradients = pullback(seq_upstream.astype(jnp.float32))
        totals = tuple((total_part + grad_part for total_part, grad_part in zip(totals, gradients[1:])))
        return (totals, (outputs.astype(jnp.bfloat16), gradients[0]))
    starting = tuple((jnp.zeros(matrix.shape, jnp.float32) for matrix in params))
    totals, results = lax.scan(scan_step, starting, (block_input, upstream))
    block_output, input_grad = results
    return (block_output, input_grad, totals[0], totals[1], totals[2], totals[3], totals[4], totals[5])
```

```python
import math

import jax
import jax.numpy as jnp
from jax import lax
from jax.experimental import pallas as pl
from jax.experimental.pallas import tpu as pltpu
from jax.sharding import PartitionSpec as P

HEAD_DIM = 64
REACH = 64
PAIR = 2 * HEAD_DIM
TILE = 128
KEYS = TILE + 2 * REACH
AXES = ("seq", "fsdp")

epsilon = 1e-05
masked_value = -1e30
f32 = jnp.float32
bf16 = jnp.bfloat16
VMEM_LIMIT = 56 * 1024 * 1024


def call(body, grid, in_specs, out_specs, out_shape, flops, moved, scratch=()):
    return pl.pallas_call(
        body,
        grid=grid,
        in_specs=in_specs,
        out_specs=out_specs,
        out_shape=out_shape,
        scratch_shapes=list(scratch),
        compiler_params=pltpu.CompilerParams(
            vmem_limit_bytes=VMEM_LIMIT,
            dimension_semantics=("arbitrary",) * len(grid),
        ),
        cost_estimate=pl.CostEstimate(flops=flops, bytes_accessed=moved, transcendentals=0),
    )


def dot_nn(a, b):
    return lax.dot_general(a, b, (((1,), (0,)), ((), ())), preferred_element_type=f32)


def dot_nt(a, b):
    return lax.dot_general(a, b, (((1,), (1,)), ((), ())), preferred_element_type=f32)


def dot_tn(a, b):
    return lax.dot_general(a, b, (((0,), (0,)), ((), ())), preferred_element_type=f32)


def low_half(shape):
    lane = lax.broadcasted_iota(jnp.int32, shape, 1)
    return (lane % HEAD_DIM) < HEAD_DIM // 2


def spin(values, cosine, sine):
    half = HEAD_DIM // 2
    turned = jnp.where(
        low_half(values.shape),
        pltpu.roll(values, PAIR - half, 1),
        pltpu.roll(values, half, 1),
    )
    return values * cosine + turned * sine


def normalized(values):
    center = values - jnp.mean(values, axis=-1, keepdims=True)
    spread = jnp.mean(center * center, axis=-1, keepdims=True)
    inverse = lax.rsqrt(spread + epsilon)
    return center * inverse, inverse


def norm_back(e, gain, xhat, inverse):
    eg = e * gain
    return (
        eg - jnp.mean(eg, axis=-1, keepdims=True) - xhat * jnp.mean(eg * xhat, axis=-1, keepdims=True)
    ) * inverse


def joint_body(x_ref, w_ref, gain_ref, cos_ref, sin_ref, normed_ref, qkv_ref):
    width = x_ref.shape[1]
    xhat, _ = normalized(x_ref[...].astype(f32))
    normed = (xhat * gain_ref[...]).astype(bf16)
    normed_ref[...] = normed
    cosine, sine = cos_ref[...], sin_ref[...]
    step = 2 * PAIR
    for col in range(0, 3 * width, step):
        out = dot_nn(normed, w_ref[:, col : col + step])
        if col < 2 * width:
            out = jnp.concatenate(
                [spin(out[:, :PAIR], cosine, sine), spin(out[:, PAIR:], cosine, sine)], axis=1
            )
            if col < width:
                out = out * (1.0 / math.sqrt(HEAD_DIM))
        qkv_ref[:, col : col + step] = out.astype(bf16)


def stacked_heads(rows):
    lane = lax.broadcasted_iota(jnp.int32, rows.shape, 1)
    zero = jnp.zeros_like(rows)
    first = jnp.where(lane < HEAD_DIM, rows, zero)
    second = jnp.where(lane < HEAD_DIM, zero, rows)
    return jnp.concatenate([first, second], axis=0)


def merged_heads(both):
    lane = lax.broadcasted_iota(jnp.int32, (TILE, PAIR), 1)
    return jnp.where(lane < HEAD_DIM, both[:TILE], both[TILE:])


def window_probs(keys, queries, bias):
    scores = dot_nt(keys, queries) + bias
    top = jnp.max(scores, axis=0, keepdims=True)
    terms = jnp.exp(scores - top)
    return terms * (1.0 / jnp.sum(terms, axis=0, keepdims=True))


def attention_body(q_ref, k_ref, v_ref, kl_ref, vl_ref, kh_ref, vh_ref, bias_ref, out_ref):
    keys = jnp.concatenate([kl_ref[0], k_ref[0], kh_ref[0]], axis=0)
    values = jnp.concatenate([vl_ref[0], v_ref[0], vh_ref[0]], axis=0)
    for tile in range(q_ref.shape[1] // TILE):
        start = tile * TILE
        queries = stacked_heads(q_ref[0, start : start + TILE, :])
        probs = window_probs(keys[start : start + KEYS], queries, bias_ref[tile])
        both = dot_tn(probs.astype(bf16), values[start : start + KEYS])
        out_ref[0, start : start + TILE, :] = merged_heads(both).astype(bf16)


def attention_back_body(
    q_ref, k_ref, v_ref, kl_ref, vl_ref, kh_ref, vh_ref, bias_ref, dc_ref, cos_ref, sin_ref,
    dj_ref, edge_ref, low_ref, high_ref, dk_ref, dv_ref,
):
    width = dj_ref.shape[2] // 3
    rows = q_ref.shape[1]
    tiles = rows // TILE
    column = pl.program_id(1) * PAIR

    def cols(base):
        return pl.ds(pl.multiple_of(base + column, PAIR), PAIR)

    cosine, sine = cos_ref[...], -sin_ref[...]
    keys = jnp.concatenate([kl_ref[0], k_ref[0], kh_ref[0]], axis=0)
    values = jnp.concatenate([vl_ref[0], v_ref[0], vh_ref[0]], axis=0)
    for tile in range(tiles):
        start = tile * TILE
        key_part = keys[start : start + KEYS]
        queries = stacked_heads(q_ref[0, start : start + TILE, :])
        cotangents = stacked_heads(dc_ref[0, start : start + TILE, :])
        probs = window_probs(key_part, queries, bias_ref[tile])
        d_probs = dot_nt(values[start : start + KEYS], cotangents)
        inner = jnp.sum(probs * d_probs, axis=0, keepdims=True)
        d_scores = (probs * (d_probs - inner)).astype(bf16)
        d_value = dot_nn(probs.astype(bf16), cotangents)
        d_key = dot_nn(d_scores, queries)
        d_query = merged_heads(dot_tn(d_scores, key_part)) * (1.0 / math.sqrt(HEAD_DIM))
        d_query = spin(d_query, cosine[start : start + TILE], sine[start : start + TILE])
        dj_ref[0, start : start + TILE, cols(0)] = d_query.astype(bf16)
        if tile == 0:
            dk_ref[:TILE, :] = d_key[:TILE]
            dv_ref[:TILE, :] = d_value[:TILE]
        else:
            dk_ref[start : start + TILE, :] += d_key[:TILE]
            dv_ref[start : start + TILE, :] += d_value[:TILE]
        dk_ref[start + TILE : start + KEYS, :] = d_key[TILE:]
        dv_ref[start + TILE : start + KEYS, :] = d_value[TILE:]
    own = slice(REACH, REACH + rows)
    dj_ref[0, :, cols(width)] = spin(dk_ref[own, :], cosine, sine).astype(bf16)
    dj_ref[0, :, cols(2 * width)] = dv_ref[own, :].astype(bf16)
    for part, base in ((dk_ref, 0), (dv_ref, width)):
        edge_ref[0, :REACH, cols(base)] = part[REACH : 2 * REACH, :]
        edge_ref[0, REACH:, cols(base)] = part[rows : rows + REACH, :]
        low_ref[0, :, cols(base)] = part[:REACH, :].astype(bf16)
        high_ref[0, :, cols(base)] = part[rows + REACH :, :].astype(bf16)


def middle_body(
    x_ref, ctx_ref, up_ref, w_ref, gain_ref,
    out_ref, mixed_ref, dctx_ref, normed_ref, hidden_ref, dexp_ref,
):
    width = x_ref.shape[1]
    ff = hidden_ref.shape[1]
    gain = gain_ref[...]
    mixing = w_ref[:, :width]
    upstream = up_ref[...]
    middle = x_ref[...].astype(f32) + dot_nn(ctx_ref[...], mixing)
    xhat, inverse = normalized(middle)
    normed = (xhat * gain).astype(bf16)
    normed_ref[...] = normed
    step = 3 * PAIR
    total = middle
    e = jnp.zeros_like(middle)
    for col in range(0, ff, step):
        gate_w = w_ref[:, width + col : width + col + step]
        up_w = w_ref[:, width + ff + col : width + ff + col + step]
        reduce_w = w_ref[:, width + 2 * ff + col : width + 2 * ff + col + step]
        gate = dot_nn(normed, gate_w)
        upward = dot_nn(normed, up_w)
        d_hidden = dot_nn(upstream, reduce_w)
        cdf = 0.5 + 0.5 * lax.erf(gate * math.sqrt(0.5))
        slope = cdf + gate * jnp.exp(-0.5 * gate * gate) * (1.0 / math.sqrt(2.0 * math.pi))
        act = gate * cdf
        hidden = (act * upward).astype(bf16)
        d_gate = (d_hidden * upward * slope).astype(bf16)
        d_up = (d_hidden * act).astype(bf16)
        hidden_ref[:, col : col + step] = hidden
        dexp_ref[:, col : col + step] = d_gate
        dexp_ref[:, ff + col : ff + col + step] = d_up
        total = total + dot_nt(hidden, reduce_w)
        e = e + dot_nt(d_gate, gate_w) + dot_nt(d_up, up_w)
    out_ref[...] = total.astype(bf16)
    d_middle = upstream.astype(f32) + norm_back(e, gain, xhat, inverse)
    mixed = d_middle.astype(bf16)
    mixed_ref[...] = mixed
    dctx_ref[...] = dot_nt(mixed, mixing).astype(bf16)


def joint_grad_body(
    dj_ref, edge_ref, below_ref, above_ref, normed_ref, cos_ref, sin_ref, out_ref, grad_ref, acc_ref
):
    width = normed_ref.shape[2]
    rows = dj_ref.shape[1]
    out_ref[0, REACH : rows - REACH, :] = dj_ref[0, REACH : rows - REACH, :]
    for source, at, came in ((0, 0, below_ref), (REACH, rows - REACH, above_ref)):
        here = slice(at, at + REACH)
        out_ref[0, here, :width] = dj_ref[0, here, :width]
        cosine, sine = cos_ref[here, :], -sin_ref[here, :]
        for col in range(0, 2 * width, PAIR):
            piece = slice(col, col + PAIR)
            total = edge_ref[0, source : source + REACH, piece] + came[0, :, piece].astype(f32)
            if col < width:
                total = spin(total, cosine, sine)
            out_ref[0, here, width + col : width + col + PAIR] = total.astype(bf16)
    index = pl.program_id(0)

    @pl.when(index == 0)
    def _():
        acc_ref[...] = jnp.zeros_like(acc_ref)

    flipped = normed_ref[0].T
    step = 2 * PAIR
    for col in range(0, 3 * width, step):
        acc_ref[:, col : col + step] += dot_nn(flipped, out_ref[0, :, col : col + step])

    @pl.when(index == pl.num_programs(0) - 1)
    def _():
        grad_ref[...] = acc_ref[...].astype(bf16)


def weight_grad_body(
    ctx_ref, mixed_ref, normed_ref, dexp_ref, up_ref, hidden_ref, grad_ref, acc_ref
):
    index = pl.program_id(0)

    @pl.when(index == 0)
    def _():
        acc_ref[...] = jnp.zeros_like(acc_ref)

    base = 0
    step = 3 * PAIR
    for left, right in ((ctx_ref, mixed_ref), (normed_ref, dexp_ref), (up_ref, hidden_ref)):
        flipped = left[...].T
        for col in range(0, right.shape[1], step):
            acc_ref[:, base + col : base + col + step] += dot_nn(
                flipped, right[:, col : col + step]
            )
        base += right.shape[1]

    @pl.when(index == pl.num_programs(0) - 1)
    def _():
        grad_ref[...] = acc_ref[...].astype(bf16)


def input_body(dj_ref, w_ref, x_ref, mixed_ref, gain_ref, out_ref):
    e = dot_nt(dj_ref[...], w_ref[:, : dj_ref.shape[1]])
    xhat, inverse = normalized(x_ref[...].astype(f32))
    out_ref[...] = mixed_ref[...].astype(f32) + norm_back(e, gain_ref[...], xhat, inverse)


def shifted(x, by):
    devices = lax.axis_size("seq")
    pairs = [(i, i + by) for i in range(devices) if 0 <= i + by < devices]
    return lax.ppermute(x, "seq", pairs)


def per_device(
    block_input, gain_before, joint_weight, mixing_weight, gain_middle, expand_weight,
    reduce_weight, upstream,
):
    seqs, piece, width = block_input.shape
    ff = reduce_weight.shape[0]
    tokens = seqs * piece
    pairs = width // PAIR
    shard = gain_before.shape[0]
    devices = lax.axis_size("seq")

    lead = jnp.concatenate(
        [
            joint_weight,
            gain_before[:, None],
            gain_middle[:, None],
            jnp.zeros((shard, PAIR - 2), bf16),
        ],
        axis=1,
    )
    lead = lax.all_gather(lead, AXES, axis=0, tiled=True)
    rest = jnp.concatenate([mixing_weight, expand_weight, reduce_weight.T], axis=1)
    rest = lax.all_gather(rest, AXES, axis=0, tiled=True)
    gain_a = lead[:, 3 * width].astype(f32)[None, :]
    gain_f = lead[:, 3 * width + 1].astype(f32)[None, :]

    place = lax.axis_index("seq")
    positions = place * piece + jnp.arange(piece, dtype=jnp.int32)
    half = HEAD_DIM // 2
    exponent = jnp.arange(half, dtype=f32) * (2.0 / HEAD_DIM)
    inverse = jnp.power(10000.0, -exponent)
    angles = positions.astype(f32)[:, None] * inverse[None, :]
    cosine, sine = jnp.cos(angles), jnp.sin(angles)
    cosine = jnp.concatenate([cosine] * 4, axis=-1)
    sine = jnp.concatenate([-sine, sine, -sine, sine], axis=-1)

    tiles = piece // TILE
    tile = jnp.arange(tiles, dtype=jnp.int32)[:, None, None]
    key = jnp.arange(KEYS, dtype=jnp.int32)[None, :, None]
    query = jnp.arange(2 * TILE, dtype=jnp.int32)[None, None, :] % TILE
    key_pos = place * piece + tile * TILE - REACH + key
    gap = key - query
    allowed = (gap >= 0) & (gap <= 2 * REACH) & (key_pos >= 0) & (key_pos < devices * piece)
    bias = jnp.where(allowed, 0.0, masked_value).astype(f32)

    block = 256
    steps = tokens // block
    per_seq = piece // block
    x_flat = block_input.reshape(tokens, width)
    up_flat = upstream.reshape(tokens, width)

    def rows(columns):
        return pl.BlockSpec((block, columns), lambda i: (i, 0))

    def whole(*shape):
        return pl.BlockSpec(shape, lambda *i: (0,) * len(shape))

    def shape(*dims, dtype=bf16):
        return jax.ShapeDtypeStruct(dims, dtype)

    table = pl.BlockSpec((block, PAIR), lambda i: (i % per_seq, 0))
    normed, qkv = call(
        joint_body,
        (steps,),
        [rows(width), whole(*lead.shape), whole(1, width), table, table],
        [rows(width), rows(3 * width)],
        [shape(tokens, width), shape(tokens, 3 * width)],
        6 * tokens * width * width,
        tokens * width * 10 + 6 * width * width,
    )(x_flat, lead, gain_a, cosine, sine)
    qkv = qkv.reshape(seqs, piece, 3 * width)

    from_below = shifted(qkv[:, piece - REACH :, width:], 1)
    from_above = shifted(qkv[:, :REACH, width:], -1)

    def heads(height, base):
        return pl.BlockSpec((1, height, PAIR), lambda g, j: (g, 0, base + j))

    window_specs = [
        heads(piece, 0),
        heads(piece, pairs),
        heads(piece, 2 * pairs),
        heads(REACH, 0),
        heads(REACH, pairs),
        heads(REACH, 0),
        heads(REACH, pairs),
        whole(*bias.shape),
    ]
    window_args = (
        qkv, qkv, qkv, from_below, from_below, from_above, from_above, bias,
    )
    attended = 4 * tokens * KEYS * width
    context = call(
        attention_body,
        (seqs, pairs),
        window_specs,
        heads(piece, 0),
        shape(seqs, piece, width),
        attended * 4,
        tokens * width * 8,
    )(*window_args)
    ctx_flat = context.reshape(tokens, width)

    block_output, mixed, d_context, normed_ffn, hidden, d_expanded = call(
        middle_body,
        (steps,),
        [rows(width), rows(width), rows(width), whole(*rest.shape), whole(1, width)],
        [rows(width), rows(width), rows(width), rows(width), rows(ff), rows(2 * ff)],
        [
            shape(tokens, width),
            shape(tokens, width),
            shape(tokens, width),
            shape(tokens, width),
            shape(tokens, ff),
            shape(tokens, 2 * ff),
        ],
        4 * tokens * width * (width + 3 * ff),
        tokens * (14 * width + 6 * ff) + rest.size * 2,
    )(x_flat, ctx_flat, up_flat, rest, gain_f)

    def summed(partial):
        return lax.psum_scatter(
            partial, AXES, scatter_dimension=0, tiled=True
        ).astype(f32)

    def tall(columns):
        return pl.BlockSpec((piece, columns), lambda i: (i, 0))

    rest_partial = call(
        weight_grad_body,
        (seqs,),
        [tall(width), tall(width), tall(width), tall(2 * ff), tall(width), tall(ff)],
        whole(*rest.shape),
        shape(*rest.shape),
        2 * tokens * width * (width + 3 * ff),
        tokens * (8 * width + 6 * ff) + rest.size * 2,
        [pltpu.VMEM(rest.shape, f32)],
    )(ctx_flat, mixed, normed_ffn, d_expanded, up_flat, hidden)
    d_context, rest_partial = lax.optimization_barrier((d_context, rest_partial))
    rest_grad = summed(rest_partial)
    wide = pl.BlockSpec((piece, PAIR), lambda g, j: (0, 0))
    d_joint, edges, low_rim, high_rim = call(
        attention_back_body,
        (seqs, pairs),
        window_specs + [heads(piece, 0), wide, wide],
        [
            pl.BlockSpec((1, piece, 3 * width), lambda g, j: (g, 0, 0)),
            pl.BlockSpec((1, 2 * REACH, 2 * width), lambda g, j: (g, 0, 0)),
            pl.BlockSpec((1, REACH, 2 * width), lambda g, j: (g, 0, 0)),
            pl.BlockSpec((1, REACH, 2 * width), lambda g, j: (g, 0, 0)),
        ],
        [
            shape(seqs, piece, 3 * width),
            shape(seqs, 2 * REACH, 2 * width, dtype=f32),
            shape(seqs, REACH, 2 * width),
            shape(seqs, REACH, 2 * width),
        ],
        attended * 10,
        tokens * width * 16,
        [pltpu.VMEM((piece + 2 * REACH, PAIR), f32)] * 2,
    )(*window_args, d_context.reshape(seqs, piece, width), cosine, sine)
    back_above = shifted(low_rim, -1)
    back_below = shifted(high_rim, 1)

    def one_seq(height, columns):
        return pl.BlockSpec((1, height, columns), lambda g: (g, 0, 0))

    d_joint, joint_partial = call(
        joint_grad_body,
        (seqs,),
        [
            one_seq(piece, 3 * width),
            one_seq(2 * REACH, 2 * width),
            one_seq(REACH, 2 * width),
            one_seq(REACH, 2 * width),
            one_seq(piece, width),
            whole(piece, PAIR),
            whole(piece, PAIR),
        ],
        [one_seq(piece, 3 * width), whole(width, 3 * width)],
        [shape(seqs, piece, 3 * width), shape(width, 3 * width)],
        6 * tokens * width * width,
        tokens * width * 14 + 6 * width * width,
        [pltpu.VMEM((width, 3 * width), f32)],
    )(d_joint, edges, back_below, back_above, normed.reshape(seqs, piece, width), cosine, sine)
    joint_partial, rest_grad = lax.optimization_barrier((joint_partial, rest_grad))
    joint_grad = summed(joint_partial)
    mixing_grad = rest_grad[:, :width]
    expand_grad = rest_grad[:, width : width + 2 * ff]
    reduce_grad = rest_grad[:, width + 2 * ff :].T

    input_grad = call(
        input_body,
        (steps,),
        [rows(3 * width), whole(*lead.shape), rows(width), rows(width), whole(1, width)],
        rows(width),
        shape(tokens, width, dtype=f32),
        6 * tokens * width * width,
        tokens * width * 14 + 6 * width * width,
    )(d_joint.reshape(tokens, 3 * width), lead, x_flat, mixed, gain_a)

    before_grad = jnp.sum(joint_weight.astype(f32) * joint_grad, axis=1) / gain_before.astype(f32)
    middle_grad = jnp.sum(expand_weight.astype(f32) * expand_grad, axis=1) / gain_middle.astype(f32)
    return (
        block_output.reshape(seqs, piece, width),
        input_grad.reshape(seqs, piece, width),
        before_grad,
        joint_grad,
        mixing_grad,
        middle_grad,
        expand_grad,
        reduce_grad,
    )


def solution(mesh):
    token = P("fsdp", "seq", None)
    vector = P(AXES)
    matrix = P(AXES, None)
    turned = P(None, AXES)
    in_specs = (token, vector, matrix, matrix, vector, matrix, turned, token)
    out_specs = (token, token, vector, matrix, matrix, vector, matrix, turned)
    return jax.shard_map(
        per_device, mesh=mesh, in_specs=in_specs, out_specs=out_specs, check_vma=False
    )
```

```python
import math

import jax
import jax.numpy as jnp
from jax import lax
from jax.experimental import pallas as pl
from jax.experimental.pallas import tpu as pltpu
from jax.sharding import PartitionSpec as P

HEAD_DIM = 64
REACH = 64
PAIR = 2 * HEAD_DIM
TILE = 128
KEYS = TILE + 2 * REACH
AXES = ("seq", "fsdp")

epsilon = 1e-05
masked_value = -1e30
f32 = jnp.float32
bf16 = jnp.bfloat16
VMEM_LIMIT = 56 * 1024 * 1024


def call(body, grid, in_specs, out_specs, out_shape, flops, moved, scratch=()):
    return pl.pallas_call(
        body,
        grid=grid,
        in_specs=in_specs,
        out_specs=out_specs,
        out_shape=out_shape,
        scratch_shapes=list(scratch),
        compiler_params=pltpu.CompilerParams(
            vmem_limit_bytes=VMEM_LIMIT,
            dimension_semantics=("arbitrary",) * len(grid),
        ),
        cost_estimate=pl.CostEstimate(flops=flops, bytes_accessed=moved, transcendentals=0),
    )


def dot_nn(a, b):
    return lax.dot_general(a, b, (((1,), (0,)), ((), ())), preferred_element_type=f32)


def dot_nt(a, b):
    return lax.dot_general(a, b, (((1,), (1,)), ((), ())), preferred_element_type=f32)


def dot_tn(a, b):
    return lax.dot_general(a, b, (((0,), (0,)), ((), ())), preferred_element_type=f32)


def low_half(shape):
    lane = lax.broadcasted_iota(jnp.int32, shape, 1)
    return (lane % HEAD_DIM) < HEAD_DIM // 2


def spin(values, cosine, sine):
    half = HEAD_DIM // 2
    turned = jnp.where(
        low_half(values.shape),
        pltpu.roll(values, PAIR - half, 1),
        pltpu.roll(values, half, 1),
    )
    return values * cosine + turned * sine


def normalized(values):
    center = values - jnp.mean(values, axis=-1, keepdims=True)
    spread = jnp.mean(center * center, axis=-1, keepdims=True)
    inverse = lax.rsqrt(spread + epsilon)
    return center * inverse, inverse


def norm_back(e, gain, xhat, inverse):
    eg = e * gain
    return (
        eg - jnp.mean(eg, axis=-1, keepdims=True) - xhat * jnp.mean(eg * xhat, axis=-1, keepdims=True)
    ) * inverse


def joint_body(x_ref, w_ref, gain_ref, cos_ref, sin_ref, normed_ref, qkv_ref):
    width = x_ref.shape[1]
    xhat, _ = normalized(x_ref[...].astype(f32))
    normed = (xhat * gain_ref[...]).astype(bf16)
    normed_ref[...] = normed
    cosine, sine = cos_ref[...], sin_ref[...]
    step = 2 * PAIR
    for col in range(0, 3 * width, step):
        out = dot_nn(normed, w_ref[:, col : col + step])
        if col < 2 * width:
            out = jnp.concatenate(
                [spin(out[:, :PAIR], cosine, sine), spin(out[:, PAIR:], cosine, sine)], axis=1
            )
            if col < width:
                out = out * (1.0 / math.sqrt(HEAD_DIM))
        qkv_ref[:, col : col + step] = out.astype(bf16)


def stacked_heads(rows):
    lane = lax.broadcasted_iota(jnp.int32, rows.shape, 1)
    zero = jnp.zeros_like(rows)
    first = jnp.where(lane < HEAD_DIM, rows, zero)
    second = jnp.where(lane < HEAD_DIM, zero, rows)
    return jnp.concatenate([first, second], axis=0)


def merged_heads(both):
    lane = lax.broadcasted_iota(jnp.int32, (TILE, PAIR), 1)
    return jnp.where(lane < HEAD_DIM, both[:TILE], both[TILE:])


def window_probs(keys, queries, bias):
    scores = dot_nt(keys, queries) + bias
    top = jnp.max(scores, axis=0, keepdims=True)
    terms = jnp.exp(scores - top)
    return terms * (1.0 / jnp.sum(terms, axis=0, keepdims=True))


def attention_body(q_ref, k_ref, v_ref, kl_ref, vl_ref, kh_ref, vh_ref, bias_ref, out_ref):
    keys = jnp.concatenate([kl_ref[0], k_ref[0], kh_ref[0]], axis=0)
    values = jnp.concatenate([vl_ref[0], v_ref[0], vh_ref[0]], axis=0)
    for tile in range(q_ref.shape[1] // TILE):
        start = tile * TILE
        queries = stacked_heads(q_ref[0, start : start + TILE, :])
        probs = window_probs(keys[start : start + KEYS], queries, bias_ref[tile])
        both = dot_tn(probs.astype(bf16), values[start : start + KEYS])
        out_ref[0, start : start + TILE, :] = merged_heads(both).astype(bf16)


def attention_back_body(
    q_ref, k_ref, v_ref, kl_ref, vl_ref, kh_ref, vh_ref, bias_ref, dc_ref, cos_ref, sin_ref,
    dj_ref, edge_ref, low_ref, high_ref, dk_ref, dv_ref,
):
    width = dj_ref.shape[2] // 3
    rows = q_ref.shape[1]
    tiles = rows // TILE
    column = pl.program_id(1) * PAIR

    def cols(base):
        return pl.ds(pl.multiple_of(base + column, PAIR), PAIR)

    cosine, sine = cos_ref[...], -sin_ref[...]
    keys = jnp.concatenate([kl_ref[0], k_ref[0], kh_ref[0]], axis=0)
    values = jnp.concatenate([vl_ref[0], v_ref[0], vh_ref[0]], axis=0)
    for tile in range(tiles):
        start = tile * TILE
        key_part = keys[start : start + KEYS]
        queries = stacked_heads(q_ref[0, start : start + TILE, :])
        cotangents = stacked_heads(dc_ref[0, start : start + TILE, :])
        probs = window_probs(key_part, queries, bias_ref[tile])
        d_probs = dot_nt(values[start : start + KEYS], cotangents)
        inner = jnp.sum(probs * d_probs, axis=0, keepdims=True)
        d_scores = (probs * (d_probs - inner)).astype(bf16)
        d_value = dot_nn(probs.astype(bf16), cotangents)
        d_key = dot_nn(d_scores, queries)
        d_query = merged_heads(dot_tn(d_scores, key_part)) * (1.0 / math.sqrt(HEAD_DIM))
        d_query = spin(d_query, cosine[start : start + TILE], sine[start : start + TILE])
        dj_ref[0, start : start + TILE, cols(0)] = d_query.astype(bf16)
        if tile == 0:
            dk_ref[:TILE, :] = d_key[:TILE]
            dv_ref[:TILE, :] = d_value[:TILE]
        else:
            dk_ref[start : start + TILE, :] += d_key[:TILE]
            dv_ref[start : start + TILE, :] += d_value[:TILE]
        dk_ref[start + TILE : start + KEYS, :] = d_key[TILE:]
        dv_ref[start + TILE : start + KEYS, :] = d_value[TILE:]
    own = slice(REACH, REACH + rows)
    dj_ref[0, :, cols(width)] = spin(dk_ref[own, :], cosine, sine).astype(bf16)
    dj_ref[0, :, cols(2 * width)] = dv_ref[own, :].astype(bf16)
    for part, base in ((dk_ref, 0), (dv_ref, width)):
        edge_ref[0, :REACH, cols(base)] = part[REACH : 2 * REACH, :]
        edge_ref[0, REACH:, cols(base)] = part[rows : rows + REACH, :]
        low_ref[0, :, cols(base)] = part[:REACH, :].astype(bf16)
        high_ref[0, :, cols(base)] = part[rows + REACH :, :].astype(bf16)


def middle_body(
    x_ref, ctx_ref, up_ref, w_ref, gain_ref,
    out_ref, mixed_ref, dctx_ref, normed_ref, hidden_ref, dexp_ref,
):
    width = x_ref.shape[1]
    ff = hidden_ref.shape[1]
    gain = gain_ref[...]
    mixing = w_ref[:, :width]
    upstream = up_ref[...]
    middle = x_ref[...].astype(f32) + dot_nn(ctx_ref[...], mixing)
    xhat, inverse = normalized(middle)
    normed = (xhat * gain).astype(bf16)
    normed_ref[...] = normed
    step = 3 * PAIR
    total = middle
    e = jnp.zeros_like(middle)
    for col in range(0, ff, step):
        gate_w = w_ref[:, width + col : width + col + step]
        up_w = w_ref[:, width + ff + col : width + ff + col + step]
        reduce_w = w_ref[:, width + 2 * ff + col : width + 2 * ff + col + step]
        gate = dot_nn(normed, gate_w)
        upward = dot_nn(normed, up_w)
        d_hidden = dot_nn(upstream, reduce_w)
        cdf = 0.5 + 0.5 * lax.erf(gate * math.sqrt(0.5))
        slope = cdf + gate * jnp.exp(-0.5 * gate * gate) * (1.0 / math.sqrt(2.0 * math.pi))
        act = gate * cdf
        hidden = (act * upward).astype(bf16)
        d_gate = (d_hidden * upward * slope).astype(bf16)
        d_up = (d_hidden * act).astype(bf16)
        hidden_ref[:, col : col + step] = hidden
        dexp_ref[:, col : col + step] = d_gate
        dexp_ref[:, ff + col : ff + col + step] = d_up
        total = total + dot_nt(hidden, reduce_w)
        e = e + dot_nt(d_gate, gate_w) + dot_nt(d_up, up_w)
    out_ref[...] = total.astype(bf16)
    d_middle = upstream.astype(f32) + norm_back(e, gain, xhat, inverse)
    mixed = d_middle.astype(bf16)
    mixed_ref[...] = mixed
    dctx_ref[...] = dot_nt(mixed, mixing).astype(bf16)


def joint_grad_body(
    dj_ref, edge_ref, below_ref, above_ref, normed_ref, cos_ref, sin_ref, out_ref, grad_ref, acc_ref
):
    width = normed_ref.shape[2]
    rows = dj_ref.shape[1]
    out_ref[0, REACH : rows - REACH, :] = dj_ref[0, REACH : rows - REACH, :]
    for source, at, came in ((0, 0, below_ref), (REACH, rows - REACH, above_ref)):
        here = slice(at, at + REACH)
        out_ref[0, here, :width] = dj_ref[0, here, :width]
        cosine, sine = cos_ref[here, :], -sin_ref[here, :]
        for col in range(0, 2 * width, PAIR):
            piece = slice(col, col + PAIR)
            total = edge_ref[0, source : source + REACH, piece] + came[0, :, piece].astype(f32)
            if col < width:
                total = spin(total, cosine, sine)
            out_ref[0, here, width + col : width + col + PAIR] = total.astype(bf16)
    index = pl.program_id(0)

    @pl.when(index == 0)
    def _():
        acc_ref[...] = jnp.zeros_like(acc_ref)

    flipped = normed_ref[0].T
    step = 2 * PAIR
    for col in range(0, 3 * width, step):
        acc_ref[:, col : col + step] += dot_nn(flipped, out_ref[0, :, col : col + step])

    @pl.when(index == pl.num_programs(0) - 1)
    def _():
        grad_ref[...] = acc_ref[...].astype(bf16)


def weight_grad_body(
    ctx_ref, mixed_ref, normed_ref, dexp_ref, up_ref, hidden_ref, grad_ref, acc_ref
):
    index = pl.program_id(0)

    @pl.when(index == 0)
    def _():
        acc_ref[...] = jnp.zeros_like(acc_ref)

    base = 0
    step = 3 * PAIR
    for left, right in ((ctx_ref, mixed_ref), (normed_ref, dexp_ref), (up_ref, hidden_ref)):
        flipped = left[...].T
        for col in range(0, right.shape[1], step):
            acc_ref[:, base + col : base + col + step] += dot_nn(
                flipped, right[:, col : col + step]
            )
        base += right.shape[1]

    @pl.when(index == pl.num_programs(0) - 1)
    def _():
        grad_ref[...] = acc_ref[...].astype(bf16)


def input_body(dj_ref, w_ref, x_ref, mixed_ref, gain_ref, out_ref):
    e = dot_nt(dj_ref[...], w_ref[:, : dj_ref.shape[1]])
    xhat, inverse = normalized(x_ref[...].astype(f32))
    out_ref[...] = mixed_ref[...].astype(f32) + norm_back(e, gain_ref[...], xhat, inverse)


def shifted(x, by):
    devices = lax.axis_size("seq")
    pairs = [(i, i + by) for i in range(devices) if 0 <= i + by < devices]
    return lax.ppermute(x, "seq", pairs)


def swap_order():
    seq = [("seq", b) for b in reversed(range(lax.axis_size("seq").bit_length() - 1))]
    fsdp = [("fsdp", b) for b in reversed(range(lax.axis_size("fsdp").bit_length() - 1))]
    return seq + fsdp, [seq[-1]] + fsdp[::-1] + seq[-2::-1]


def swapped(x, axis, bit):
    return lax.ppermute(x, axis, [(i, i ^ (1 << bit)) for i in range(lax.axis_size(axis))])


def scattered_sum(partial, earlier):
    left, order = swap_order()
    rows = partial.shape[0] >> len(left)
    part = partial.reshape((2,) * len(left) + (rows, partial.shape[1]))
    for axis, bit in order:
        dim = left.index((axis, bit))
        left.remove((axis, bit))
        mine = (lax.axis_index(axis) >> bit) & 1
        zero = lax.index_in_dim(part, 0, dim, keepdims=False)
        one = lax.index_in_dim(part, 1, dim, keepdims=False)
        kept = jnp.where(mine == 0, zero, one).astype(f32)
        sent = jnp.where(mine == 0, one, zero).astype(bf16)
        part = kept + swapped(sent, axis, bit).astype(f32)
        if (axis, bit) == order[0]:
            part, earlier = lax.optimization_barrier((part, earlier))
    return part, earlier


def gathered_rows(shard):
    ranked, order = swap_order()
    done = []
    part = shard
    for axis, bit in order[::-1]:
        mine = (lax.axis_index(axis) >> bit) & 1
        other = swapped(part, axis, bit)
        zero = jnp.where(mine == 0, part, other)
        one = jnp.where(mine == 0, other, part)
        rank = ranked.index((axis, bit))
        part = jnp.stack([zero, one], axis=sum(r < rank for r in done))
        done.append(rank)
    return part.reshape(-1, shard.shape[1])


def per_device(
    block_input, gain_before, joint_weight, mixing_weight, gain_middle, expand_weight,
    reduce_weight, upstream,
):
    seqs, piece, width = block_input.shape
    ff = reduce_weight.shape[0]
    tokens = seqs * piece
    pairs = width // PAIR
    shard = gain_before.shape[0]
    devices = lax.axis_size("seq")

    lead = jnp.concatenate(
        [
            joint_weight,
            gain_before[:, None],
            gain_middle[:, None],
            jnp.zeros((shard, PAIR - 2), bf16),
        ],
        axis=1,
    )
    lead = gathered_rows(lead)
    rest = jnp.concatenate([mixing_weight, expand_weight, reduce_weight.T], axis=1)
    rest = lax.all_gather(rest, AXES, axis=0, tiled=True)
    gain_a = lead[:, 3 * width].astype(f32)[None, :]
    gain_f = lead[:, 3 * width + 1].astype(f32)[None, :]

    place = lax.axis_index("seq")
    positions = place * piece + jnp.arange(piece, dtype=jnp.int32)
    half = HEAD_DIM // 2
    exponent = jnp.arange(half, dtype=f32) * (2.0 / HEAD_DIM)
    inverse = jnp.power(10000.0, -exponent)
    angles = positions.astype(f32)[:, None] * inverse[None, :]
    cosine, sine = jnp.cos(angles), jnp.sin(angles)
    cosine = jnp.concatenate([cosine] * 4, axis=-1)
    sine = jnp.concatenate([-sine, sine, -sine, sine], axis=-1)

    tiles = piece // TILE
    tile = jnp.arange(tiles, dtype=jnp.int32)[:, None, None]
    key = jnp.arange(KEYS, dtype=jnp.int32)[None, :, None]
    query = jnp.arange(2 * TILE, dtype=jnp.int32)[None, None, :] % TILE
    key_pos = place * piece + tile * TILE - REACH + key
    gap = key - query
    allowed = (gap >= 0) & (gap <= 2 * REACH) & (key_pos >= 0) & (key_pos < devices * piece)
    bias = jnp.where(allowed, 0.0, masked_value).astype(f32)

    block = 256
    steps = tokens // block
    per_seq = piece // block
    x_flat = block_input.reshape(tokens, width)
    up_flat = upstream.reshape(tokens, width)

    def rows(columns):
        return pl.BlockSpec((block, columns), lambda i: (i, 0))

    def whole(*shape):
        return pl.BlockSpec(shape, lambda *i: (0,) * len(shape))

    def shape(*dims, dtype=bf16):
        return jax.ShapeDtypeStruct(dims, dtype)

    table = pl.BlockSpec((block, PAIR), lambda i: (i % per_seq, 0))
    normed, qkv = call(
        joint_body,
        (steps,),
        [rows(width), whole(*lead.shape), whole(1, width), table, table],
        [rows(width), rows(3 * width)],
        [shape(tokens, width), shape(tokens, 3 * width)],
        6 * tokens * width * width,
        tokens * width * 10 + 6 * width * width,
    )(x_flat, lead, gain_a, cosine, sine)
    qkv = qkv.reshape(seqs, piece, 3 * width)

    from_below = shifted(qkv[:, piece - REACH :, width:], 1)
    from_above = shifted(qkv[:, :REACH, width:], -1)

    def heads(height, base):
        return pl.BlockSpec((1, height, PAIR), lambda g, j: (g, 0, base + j))

    window_specs = [
        heads(piece, 0),
        heads(piece, pairs),
        heads(piece, 2 * pairs),
        heads(REACH, 0),
        heads(REACH, pairs),
        heads(REACH, 0),
        heads(REACH, pairs),
        whole(*bias.shape),
    ]
    window_args = (
        qkv, qkv, qkv, from_below, from_below, from_above, from_above, bias,
    )
    attended = 4 * tokens * KEYS * width
    context = call(
        attention_body,
        (seqs, pairs),
        window_specs,
        heads(piece, 0),
        shape(seqs, piece, width),
        attended * 4,
        tokens * width * 8,
    )(*window_args)
    ctx_flat = context.reshape(tokens, width)

    block_output, mixed, d_context, normed_ffn, hidden, d_expanded = call(
        middle_body,
        (steps,),
        [rows(width), rows(width), rows(width), whole(*rest.shape), whole(1, width)],
        [rows(width), rows(width), rows(width), rows(width), rows(ff), rows(2 * ff)],
        [
            shape(tokens, width),
            shape(tokens, width),
            shape(tokens, width),
            shape(tokens, width),
            shape(tokens, ff),
            shape(tokens, 2 * ff),
        ],
        4 * tokens * width * (width + 3 * ff),
        tokens * (14 * width + 6 * ff) + rest.size * 2,
    )(x_flat, ctx_flat, up_flat, rest, gain_f)

    def summed(partial):
        return lax.psum_scatter(
            partial, AXES, scatter_dimension=0, tiled=True
        ).astype(f32)

    def tall(columns):
        return pl.BlockSpec((piece, columns), lambda i: (i, 0))

    rest_partial = call(
        weight_grad_body,
        (seqs,),
        [tall(width), tall(width), tall(width), tall(2 * ff), tall(width), tall(ff)],
        whole(*rest.shape),
        shape(*rest.shape),
        2 * tokens * width * (width + 3 * ff),
        tokens * (8 * width + 6 * ff) + rest.size * 2,
        [pltpu.VMEM(rest.shape, f32)],
    )(ctx_flat, mixed, normed_ffn, d_expanded, up_flat, hidden)
    d_context, rest_partial = lax.optimization_barrier((d_context, rest_partial))
    rest_grad = summed(rest_partial)
    wide = pl.BlockSpec((piece, PAIR), lambda g, j: (0, 0))
    d_joint, edges, low_rim, high_rim = call(
        attention_back_body,
        (seqs, pairs),
        window_specs + [heads(piece, 0), wide, wide],
        [
            pl.BlockSpec((1, piece, 3 * width), lambda g, j: (g, 0, 0)),
            pl.BlockSpec((1, 2 * REACH, 2 * width), lambda g, j: (g, 0, 0)),
            pl.BlockSpec((1, REACH, 2 * width), lambda g, j: (g, 0, 0)),
            pl.BlockSpec((1, REACH, 2 * width), lambda g, j: (g, 0, 0)),
        ],
        [
            shape(seqs, piece, 3 * width),
            shape(seqs, 2 * REACH, 2 * width, dtype=f32),
            shape(seqs, REACH, 2 * width),
            shape(seqs, REACH, 2 * width),
        ],
        attended * 10,
        tokens * width * 16,
        [pltpu.VMEM((piece + 2 * REACH, PAIR), f32)] * 2,
    )(*window_args, d_context.reshape(seqs, piece, width), cosine, sine)
    back_above = shifted(low_rim, -1)
    back_below = shifted(high_rim, 1)

    def one_seq(height, columns):
        return pl.BlockSpec((1, height, columns), lambda g: (g, 0, 0))

    d_joint, joint_partial = call(
        joint_grad_body,
        (seqs,),
        [
            one_seq(piece, 3 * width),
            one_seq(2 * REACH, 2 * width),
            one_seq(REACH, 2 * width),
            one_seq(REACH, 2 * width),
            one_seq(piece, width),
            whole(piece, PAIR),
            whole(piece, PAIR),
        ],
        [one_seq(piece, 3 * width), whole(width, 3 * width)],
        [shape(seqs, piece, 3 * width), shape(width, 3 * width)],
        6 * tokens * width * width,
        tokens * width * 14 + 6 * width * width,
        [pltpu.VMEM((width, 3 * width), f32)],
    )(d_joint, edges, back_below, back_above, normed.reshape(seqs, piece, width), cosine, sine)
    joint_grad, rest_grad = scattered_sum(joint_partial, rest_grad)
    mixing_grad = rest_grad[:, :width]
    expand_grad = rest_grad[:, width : width + 2 * ff]
    reduce_grad = rest_grad[:, width + 2 * ff :].T

    input_grad = call(
        input_body,
        (steps,),
        [rows(3 * width), whole(*lead.shape), rows(width), rows(width), whole(1, width)],
        rows(width),
        shape(tokens, width, dtype=f32),
        6 * tokens * width * width,
        tokens * width * 14 + 6 * width * width,
    )(d_joint.reshape(tokens, 3 * width), lead, x_flat, mixed, gain_a)

    before_grad = jnp.sum(joint_weight.astype(f32) * joint_grad, axis=1) / gain_before.astype(f32)
    middle_grad = jnp.sum(expand_weight.astype(f32) * expand_grad, axis=1) / gain_middle.astype(f32)
    return (
        block_output.reshape(seqs, piece, width),
        input_grad.reshape(seqs, piece, width),
        before_grad,
        joint_grad,
        mixing_grad,
        middle_grad,
        expand_grad,
        reduce_grad,
    )


def solution(mesh):
    token = P("fsdp", "seq", None)
    vector = P(AXES)
    matrix = P(AXES, None)
    turned = P(None, AXES)
    in_specs = (token, vector, matrix, matrix, vector, matrix, turned, token)
    out_specs = (token, token, vector, matrix, matrix, vector, matrix, turned)
    return jax.shard_map(
        per_device, mesh=mesh, in_specs=in_specs, out_specs=out_specs, check_vma=False
    )
```
